32 devices in a mesh: dp: 8 (over z, x), mp: 4 (over y, core).
Axes of the slice: x: 2, y: 2, z: 4, core: 2. Of those that a mesh axis runs over, the one named last changes fastest.
Arguments:
- acts: bfloat16 [16384, 768], P('dp'), may hold values from -6 to 6
- out_grads: bfloat16 [16384, 3072], P('dp', 'mp'), may hold values from -0.046875 to 0.046875
- block_owner: int32 [4], replicated, may hold values from 0 to 3, as said below
- left_stat: float32 [8, 768, 768], P('mp', 'dp')
- right_stat: float32 [8, 768, 768], P('mp', 'dp')
- left_root: bfloat16 [8, 768, 768], P('mp', 'dp')
- right_root: bfloat16 [8, 768, 768], P('mp', 'dp')
Outputs:
- update: bfloat16 [768, 3072], P('dp', 'mp')
- left_new: float32 [8, 768, 768], P('mp', 'dp')
- right_new: float32 [8, 768, 768], P('mp', 'dp')
The draws below stay inside these ranges and needn't reach their ends.
Inputs may be any that keep to these rules, and one draw needn't show every extreme that they name: Block c of the 4 blocks is owned by block_owner[c]; no owner holds more than 2 blocks, and some owner holds exactly 2.
All inputs are finite; a program needn't handle non-finite values.
Results may differ from the reference program's by a relative error of at most 0.0058.
Values may be sent and summed in bfloat16 or wider, within the bound.
A program may use at most 64 MiB of HBM per device.

```python
import math
import jax
import jax.numpy as jnp
from jax import lax

BLK = 768
CAP = 2
TOKENS = 16384
N_MP = 4


def symmetric_blocks(key, block_count, matrix_order, low_level, high_level, spread, tilt_low, tilt_high):
    jitter_key, level_key, tilt_key = jax.random.split(key, 3)
    jitter = jax.random.truncated_normal(jitter_key, -4.0, 4.0, (block_count, matrix_order, matrix_order), jnp.float32)
    jitter = (jitter + jnp.swapaxes(jitter, 1, 2)) * (spread / math.sqrt(2.0 * matrix_order))
    tilt_scale = jnp.exp(jax.random.uniform(tilt_key, (block_count, matrix_order), jnp.float32, math.log(tilt_low), math.log(tilt_high)))
    jitter = jitter * tilt_scale[:, :, None] * tilt_scale[:, None, :]
    levels = jnp.exp(jax.random.uniform(level_key, (block_count, matrix_order), jnp.float32, math.log(low_level), math.log(high_level)))
    diagonal_mask = jnp.eye(matrix_order, dtype=bool)
    return jnp.where(diagonal_mask[None, :, :], levels[:, :, None], jitter)


def draw_block_owner(key, part):
    key = jax.random.fold_in(key, 11)
    first_key, second_key, third_key = jax.random.split(key, 3)
    owner_order = jax.random.permutation(first_key, N_MP)
    doubled = jax.random.randint(second_key, (), 1, N_MP // 2 + 1)
    positions = jnp.arange(N_MP, dtype=jnp.int32)
    source = jnp.where(positions >= N_MP - doubled, positions - (N_MP - doubled), positions)
    assigned = owner_order[source]
    shuffle = jax.random.permutation(third_key, N_MP)
    return assigned[shuffle].astype(jnp.int32)


def draw_left_stat(key, part):
    key = jax.random.fold_in(key, 21)
    tilt_low, tilt_high = (1.0, 1.0)
    return symmetric_blocks(key, N_MP * CAP, BLK, 1.0, 2.0, 0.3, tilt_low, tilt_high)


def draw_right_stat(key, part):
    key = jax.random.fold_in(key, 22)
    tilt_low, tilt_high = (1.0, 1.0)
    return symmetric_blocks(key, N_MP * CAP, BLK, 1.0, 2.0, 0.3, tilt_low, tilt_high)


def draw_left_root(key, part):
    key = jax.random.fold_in(key, 23)
    tilt_low, tilt_high = (1.0, 1.0)
    return symmetric_blocks(key, N_MP * CAP, BLK, 1.0, 1.6, 0.4, tilt_low, tilt_high).astype(jnp.bfloat16)


def draw_right_root(key, part):
    key = jax.random.fold_in(key, 24)
    tilt_low, tilt_high = (1.0, 1.0)
    return symmetric_blocks(key, N_MP * CAP, BLK, 1.0, 1.6, 0.4, tilt_low, tilt_high).astype(jnp.bfloat16)


def spiked(drawn, rng, source, target, shards_of, factor):
    owner, partner = [(jnp.arange(drawn.shape[position]) // (drawn.shape[position] // shards_of)).reshape([-1 if axis == position else 1 for axis in range(drawn.ndim)]) for position in (source, target)]
    chosen = jax.random.permutation(rng, shards_of)[partner]
    strong = (owner == chosen) | (owner == (partner + shards_of // 2) % shards_of)
    return jnp.where(strong, factor * drawn, drawn)


def block_scale(key, shape, pieces, least, top_value):
    factor_of, own = 1.0, jax.random.fold_in(key, 6)
    for position, blocks in pieces:
        draws = jnp.exp(jax.random.uniform(jax.random.fold_in(own, position), (blocks,), jnp.float32, least / len(pieces), top_value / len(pieces)))
        factor_of = factor_of * jnp.repeat(draws, shape[position] // blocks).reshape([-1 if axis == position else 1 for axis in range(len(shape))])
    return factor_of


def scatter_about(key, shape, scale, limit, shards=(), kind=jnp.bfloat16):
    loudness = block_scale(key, shape, shards, -0.22, 0.18) if shards else 1.0
    entries = jax.random.normal(key, shape, jnp.float32) * scale * loudness
    return jnp.minimum(jnp.maximum(entries, -limit), limit).astype(kind)


def heavy_noise(stream_key, shape, scale, most, pieces, heavy, held_as=jnp.bfloat16):
    entries = scale * jax.random.normal(stream_key, shape, jnp.float32)
    if pieces:
        entries = entries * block_scale(stream_key, shape, pieces, -0.22, 0.18)
    return jnp.clip(spiked(entries, jax.random.fold_in(stream_key, 3), *heavy), -most, most).astype(held_as)


def setup_inputs(seed: int = 0) -> dict:
    arg_keys = jax.random.split(jax.random.key(seed), 8)
    return {
        "acts": heavy_noise(arg_keys[0], (TOKENS, BLK), 1.0, 6.0, ((0, 8),), (0, 1, 8, 2.0)),
        "out_grads": scatter_about(arg_keys[1], (TOKENS, N_MP * BLK), TOKENS ** -0.5, 0.046875, ((0, 8), (1, 4))),
        "block_owner": draw_block_owner(jax.random.fold_in(arg_keys[7], 71), 0),
        "left_stat": draw_left_stat(jax.random.fold_in(arg_keys[7], 71), 0),
        "right_stat": draw_right_stat(jax.random.fold_in(arg_keys[7], 71), 0),
        "left_root": draw_left_root(jax.random.fold_in(arg_keys[7], 71), 0),
        "right_root": draw_right_root(jax.random.fold_in(arg_keys[7], 71), 0),
    }


def reference(acts, out_grads, block_owner, left_stat, right_stat, left_root, right_root):
    gradient = jnp.dot(acts.T, out_grads, preferred_element_type=jnp.float32).astype(jnp.bfloat16)
    blocks = jnp.transpose(gradient.reshape(BLK, N_MP, BLK), (1, 0, 2))
    column_ids = jnp.arange(N_MP, dtype=jnp.int32)
    same_owner = block_owner[None, :] == block_owner[:, None]
    earlier = column_ids[None, :] < column_ids[:, None]
    slot_rank = jnp.sum((same_owner & earlier).astype(jnp.int32), axis=1)
    target = (block_owner * CAP + slot_rank).astype(jnp.int32)
    widened = blocks.astype(jnp.float32)
    left_gram = jnp.einsum('cik,cjk->cij', widened, widened, precision=lax.Precision.HIGHEST)
    right_gram = jnp.einsum('cki,ckj->cij', widened, widened, precision=lax.Precision.HIGHEST)
    left_rows = jnp.take(left_root, target, axis=0).astype(jnp.float32)
    right_full = jnp.take(right_root, target, axis=0).astype(jnp.float32)
    precond_left = jnp.einsum('cik,ckj->cij', left_rows, widened, precision=lax.Precision.HIGHEST).astype(jnp.bfloat16)
    finished = jnp.einsum('cik,ckj->cij', precond_left.astype(jnp.float32), right_full, precision=lax.Precision.HIGHEST).astype(jnp.bfloat16)
    update = jnp.transpose(finished, (1, 0, 2)).reshape(BLK, N_MP * BLK)
    slot_match = target[None, :] == jnp.arange(N_MP * CAP, dtype=jnp.int32)[:, None]
    slot_used = jnp.any(slot_match, axis=1)
    slot_hits = slot_match.astype(jnp.float32)
    left_pick = jnp.einsum('sc,cij->sij', slot_hits, left_gram, precision=lax.Precision.HIGHEST)
    right_pick = jnp.einsum('sc,cij->sij', slot_hits, right_gram, precision=lax.Precision.HIGHEST)
    keep_mask = slot_used[:, None, None]
    left_new = jnp.where(keep_mask, 0.8 * left_stat + 0.2 * (left_pick / BLK), left_stat)
    right_new = jnp.where(keep_mask, 0.8 * right_stat + 0.2 * (right_pick / BLK), right_stat)
    return (update, left_new, right_new)
```

```python
import functools

import jax
import jax.numpy as jnp
from jax import lax
from jax.experimental import pallas as pl
from jax.experimental.pallas import tpu as pltpu
from jax.sharding import PartitionSpec as P


def state_index(block_owner, capacity):
    block_count = block_owner.shape[0]
    column_ids = jnp.arange(block_count, dtype=jnp.int32)
    same_owner = block_owner[None, :] == block_owner[:, None]
    earlier = column_ids[None, :] < column_ids[:, None]
    slot_rank = jnp.sum((same_owner & earlier).astype(jnp.int32), axis=1)
    return block_owner * capacity + slot_rank


def owner_hits(target, owner_index, capacity):
    wanted = owner_index * capacity + jnp.arange(capacity, dtype=jnp.int32)
    return target[None, :] == wanted[:, None]


def gram_rows(own_rows, own_cols, whole_grad):
    left_part = jnp.einsum("sik,sjk->sij", own_rows, whole_grad, preferred_element_type=jnp.float32)
    right_part = jnp.einsum(
        "ski,skj->sij", own_cols, whole_grad, preferred_element_type=jnp.float32
    )
    return (left_part, right_part)


def precondition(root_rows, whole_grad, whole_right):
    left_part = jnp.einsum(
        "sik,skj->sij", root_rows, whole_grad, preferred_element_type=jnp.float32
    ).astype(jnp.bfloat16)
    return jnp.einsum(
        "sik,skj->sij", left_part, whole_right, preferred_element_type=jnp.float32
    ).astype(jnp.bfloat16)


def route_slots(slot_match, slots):
    picker = jnp.transpose(slot_match).astype(jnp.bfloat16)
    return jnp.einsum("ds,sij->dij", picker, slots, preferred_element_type=jnp.float32).astype(
        jnp.bfloat16
    )


def collective_local(acts, out_grads, block_owner, left_stat, right_stat, left_root, right_root):
    block_order = acts.shape[1]
    slab_rows = block_order // lax.axis_size("dp")
    capacity = left_stat.shape[0]
    target = state_index(block_owner, capacity)
    column_index = lax.axis_index("mp")
    slab_start = lax.axis_index("dp") * slab_rows
    my_owner = block_owner[column_index]
    own_grad = lax.psum_scatter(
        jnp.einsum("tr,tc->rc", acts, out_grads, preferred_element_type=jnp.float32),
        "dp",
        scatter_dimension=0,
        tiled=True,
    ).astype(jnp.bfloat16)
    slot_match = owner_hits(target, column_index, capacity)
    slot_used = jnp.any(slot_match, axis=1)
    slot_weights = slot_match.astype(jnp.float32)
    left_out = route_slots(slot_match, left_root)
    right_out = route_slots(slot_match, right_root)
    left_arrived, right_arrived = (
        lax.all_to_all(left_out, "mp", split_axis=0, concat_axis=0, tiled=True),
        lax.all_to_all(right_out, "mp", split_axis=0, concat_axis=0, tiled=True),
    )
    root_rows = lax.dynamic_index_in_dim(left_arrived, my_owner, 0, keepdims=True)
    right_rows = lax.dynamic_index_in_dim(right_arrived, my_owner, 0, keepdims=True)
    whole_grad, whole_right = (
        lax.all_gather(own_grad[None], "dp", axis=1, tiled=True),
        lax.all_gather(right_rows, "dp", axis=1, tiled=True),
    )
    own_cols = lax.dynamic_slice_in_dim(whole_grad, slab_start, slab_rows, 2)
    left_part, right_part = gram_rows(own_grad[None], own_cols, whole_grad)
    update = precondition(root_rows, whole_grad, whole_right)[0]
    owner_ids = jnp.arange(block_owner.shape[0], dtype=jnp.int32)
    send_mask = (owner_ids == my_owner)[:, None, None]
    left_send = jnp.where(send_mask, left_part, 0.0)
    right_send = jnp.where(send_mask, right_part, 0.0)
    left_every_gram, right_every_gram = (
        lax.all_to_all(
            left_send.astype(jnp.bfloat16), "mp", split_axis=0, concat_axis=0, tiled=True
        ).astype(left_send.dtype),
        lax.all_to_all(
            right_send.astype(jnp.bfloat16), "mp", split_axis=0, concat_axis=0, tiled=True
        ).astype(right_send.dtype),
    )
    left_gram = jnp.einsum(
        "sc,cij->sij", slot_weights, left_every_gram, precision=lax.Precision.HIGHEST
    )
    right_gram = jnp.einsum(
        "sc,cij->sij", slot_weights, right_every_gram, precision=lax.Precision.HIGHEST
    )
    keep_mask = slot_used[:, None, None]
    left_new = jnp.where(keep_mask, 0.8 * left_stat + 0.2 * (left_gram / block_order), left_stat)
    right_new = jnp.where(
        keep_mask, 0.8 * right_stat + 0.2 * (right_gram / block_order), right_stat
    )
    return (update, left_new, right_new)


MESH = pl.DeviceIdType.MESH
BF16 = jnp.bfloat16
F32 = jnp.float32
NN = (((1,), (0,)), ((), ()))
NT = (((1,), (1,)), ((), ()))
TN = (((0,), (0,)), ((), ()))
CHUNKS = 4


def fits_fused(sizes):
    return sizes["dp"] == 8 and sizes["mp"] == 4


def flip(index, bits):
    if bits == 0:
        return index
    if bits == 1:
        return index + 1 - 2 * lax.rem(index, 2)
    if bits == 2:
        return lax.rem(index + 2, 4)
    return 3 - index


def dot(a, b, dims):
    return lax.dot_general(a, b, dims, preferred_element_type=F32)


def fused_kernel(
    owner_ref, acts_hbm, outg_hbm, left_stat_hbm, right_stat_hbm, left_root_hbm, right_root_hbm,
    update_ref, left_new_ref, right_new_ref,
    acts, outg, lstat, rstat, lroot, rroot,
    part, send_x, recv_x, send_z, recv_z, grad, right,
    lout, rout, larr, rarr, lgram, rgram,
    load_sem, tok_sem, route_ss, route_rs, rsx_ss, rsx_rs, rsz_ss, rsz_rs,
    agz_ss, agz_rs, agx_ss, agx_rs, gram_ss, gram_rs,
):
    blocks = owner_ref.shape[0]
    order = part.shape[0]
    capacity, slab = lstat.shape[0], lstat.shape[1]
    half = order // 2
    chunk = acts.shape[0] // CHUNKS
    d, m = lax.axis_index("dp"), lax.axis_index("mp")
    z, x = d // 2, lax.rem(d, 2)

    def dp_id(zz, xx):
        return {"dp": zz * 2 + xx}

    def rows_of(zz, xx):
        return pl.ds(pl.multiple_of((zz * 2 + xx) * slab, slab), slab)

    def remote(src, dst, ss, rs, device):
        return pltpu.make_async_remote_copy(
            src_ref=src, dst_ref=dst, send_sem=ss, recv_sem=rs, device_id=device, device_id_type=MESH
        )

    loads = [
        pltpu.make_async_copy(right_root_hbm, rroot, load_sem.at[0]),
        pltpu.make_async_copy(left_root_hbm, lroot, load_sem.at[1]),
    ]
    for copy in loads:
        copy.start()
    tokens = []
    for t in range(CHUNKS):
        rows = pl.ds(t * chunk, chunk)
        pair = (
            pltpu.make_async_copy(acts_hbm.at[rows], acts.at[rows], tok_sem.at[t, 0]),
            pltpu.make_async_copy(outg_hbm.at[rows], outg.at[rows], tok_sem.at[t, 1]),
        )
        for copy in pair:
            copy.start()
        tokens.append(pair)
    stats = [
        pltpu.make_async_copy(left_stat_hbm, lstat, load_sem.at[2]),
        pltpu.make_async_copy(right_stat_hbm, rstat, load_sem.at[3]),
    ]
    for copy in stats:
        copy.start()

    barrier = pltpu.get_barrier_semaphore()
    partners = [dp_id(z, 1 - x)] + [dp_id(flip(z, j), x) for j in (1, 2, 3)]
    partners += [{"mp": flip(m, j)} for j in (1, 2, 3)]
    for device in partners:
        pl.semaphore_signal(barrier, inc=1, device_id=device, device_id_type=MESH)

    owners = [owner_ref[c] for c in range(blocks)]

    def rank_of(c):
        own = owner_ref[c]
        rank = jnp.int32(0)
        for other in range(blocks):
            hit = jnp.logical_and(owners[other] == own, other < c)
            rank = rank + jnp.where(hit, 1, 0).astype(jnp.int32)
        return jnp.minimum(rank, capacity - 1)

    loads[0].wait()
    loads[1].wait()
    pl.semaphore_wait(barrier, len(partners))
    pending = []

    def start(copy):
        copy.start()
        pending.append(copy)
        return copy

    routes = {}
    for k, (root, out, arr) in enumerate(((rroot, rout, rarr), (lroot, lout, larr))):
        for j in (2, 3, 1):
            c = flip(m, j)
            out[j] = root[rank_of(c)]
            routes[k, j] = start(
                remote(out.at[j], arr.at[m], route_ss.at[k, j], route_rs.at[k, j], {"mp": c})
            )
        arr[m] = root[rank_of(m)]

    part[...] = jnp.zeros_like(part)
    partner = dp_id(z, 1 - x)
    sum_x = {}
    for step in range(2):
        which = 1 - z // 2 if step == 0 else z // 2
        base = pl.multiple_of(which * half, half)
        if step == 0:
            for t in range(CHUNKS):
                for copy in tokens[t]:
                    copy.wait()

        def token_step(t, carry):
            rows = pl.ds(pl.multiple_of(t * chunk, chunk), chunk)
            part[pl.ds(base, half), :] += dot(acts[rows, pl.ds(base, half)], outg[rows, :], TN)
            return carry

        lax.fori_loop(0, CHUNKS, token_step, 0)
        for j in ((2, 3), (1, 0))[step]:
            send_x[j] = part[rows_of(flip(z, j), 1 - x), :].astype(BF16)
            sum_x[j] = start(
                remote(send_x.at[j], recv_x.at[j], rsx_ss.at[j], rsx_rs.at[j], partner)
            )

    me = rows_of(z, x)

    def gather_own(k, ref):
        copies = {"x0": start(remote(ref.at[me], ref.at[me], agx_ss.at[k, 0], agx_rs.at[k, 0], partner))}
        for j in (2, 3, 1):
            copies[j] = start(
                remote(ref.at[me], ref.at[me], agz_ss.at[k, j], agz_rs.at[k, j], dp_id(flip(z, j), x))
            )
        return copies

    def gather_on(k, ref, copies):
        for j in (1, 2, 3):
            copies[j].wait_recv()
            rows = rows_of(flip(z, j), x)
            copies["x%d" % j] = start(
                remote(ref.at[rows], ref.at[rows], agx_ss.at[k, j], agx_rs.at[k, j], partner)
            )

    for j in (1, 2, 3):
        routes[0, j].wait_recv()
    right[me, :] = rarr[owner_ref[m]]
    right_copies = gather_own(1, right)

    sum_z = {}
    for j in (2, 3, 1):
        sum_x[j].wait_recv()
        send_z[j] = (part[rows_of(flip(z, j), x), :] + recv_x[j].astype(F32)).astype(BF16)
        sum_z[j] = start(
            remote(send_z.at[j], recv_z.at[j], rsz_ss.at[j], rsz_rs.at[j], dp_id(flip(z, j), x))
        )
    gather_on(1, right, right_copies)
    sum_x[0].wait_recv()
    total = part[me, :] + recv_x[0].astype(F32)
    for j in (1, 2, 3):
        sum_z[j].wait_recv()
        total = total + recv_z[j].astype(F32)
    own_grad = total.astype(BF16)
    grad[me, :] = own_grad
    copies = gather_own(0, grad)
    gather_on(0, grad, copies)
    for j in range(4):
        copies["x%d" % j].wait_recv()

    whole = grad[...]
    gram_copies = {}

    def share(k, ref):
        gram_copies[k, 0] = start(
            remote(ref.at[m], ref.at[m], gram_ss.at[k, 0], gram_rs.at[k, 0], {"mp": flip(m, 2)})
        )
        gram_copies[k, 1] = start(
            remote(ref.at[m], ref.at[m], gram_ss.at[k, 1], gram_rs.at[k, 1], {"mp": flip(m, 1)})
        )

    lgram[m] = dot(own_grad, whole, NT).astype(BF16)
    share(0, lgram)
    row_ids = lax.broadcasted_iota(jnp.int32, (slab, order), 0)
    col_ids = lax.broadcasted_iota(jnp.int32, (slab, order), 1)
    picker = jnp.where(col_ids == row_ids + d * slab, 1.0, 0.0).astype(BF16)
    own_cols = dot(picker, whole, NT).astype(BF16)
    rgram[m] = dot(own_cols, whole, NN).astype(BF16)
    share(1, rgram)
    for j in (1, 2, 3):
        routes[1, j].wait_recv()
    precond = dot(larr[owner_ref[m]], whole, NN).astype(BF16)
    across = flip(m, 2)
    for k, ref in ((0, lgram), (1, rgram)):
        gram_copies[k, 0].wait_recv()
        gram_copies[k, 2] = start(
            remote(ref.at[across], ref.at[across], gram_ss.at[k, 2], gram_rs.at[k, 2], {"mp": flip(m, 1)})
        )
    for j in range(4):
        right_copies["x%d" % j].wait_recv()
    update_ref[...] = dot(precond, right[...], NN).astype(BF16)

    picks = []
    for s in range(capacity):
        index, used = jnp.int32(0), jnp.int32(0)
        for c in range(blocks):
            hit = jnp.logical_and(owners[c] == m, rank_of(c) == s)
            index = index + jnp.where(hit, c, 0).astype(jnp.int32)
            used = used + jnp.where(hit, 1, 0).astype(jnp.int32)
        picks.append((jnp.minimum(index, blocks - 1), used))
    for k, (ref, stat, new) in enumerate(((lgram, lstat, left_new_ref), (rgram, rstat, right_new_ref))):
        stats[k].wait()
        gram_copies[k, 1].wait_recv()
        gram_copies[k, 2].wait_recv()
        for s, (index, used) in enumerate(picks):
            old = stat[s]
            fresh = 0.8 * old + 0.2 * (ref[index].astype(F32) / order)
            new[s] = jnp.where(used > 0, fresh, old)
    for copy in pending:
        copy.wait_send()


def fused_local(acts, out_grads, block_owner, left_stat, right_stat, left_root, right_root):
    capacity, slab, order = left_stat.shape
    blocks = block_owner.shape[0]
    tokens = acts.shape[0]
    width = out_grads.shape[1]
    dma, vmem = pltpu.SemaphoreType.DMA, pltpu.VMEM
    any_spec = pl.BlockSpec(memory_space=pl.ANY)
    vmem_spec = pl.BlockSpec(memory_space=pltpu.VMEM)
    return pl.pallas_call(
        fused_kernel,
        out_shape=(
            jax.ShapeDtypeStruct((slab, width), BF16),
            jax.ShapeDtypeStruct(left_stat.shape, F32),
            jax.ShapeDtypeStruct(right_stat.shape, F32),
        ),
        in_specs=[pl.BlockSpec(memory_space=pltpu.SMEM)] + [any_spec] * 6,
        out_specs=(vmem_spec,) * 3,
        scratch_shapes=[
            vmem((tokens, order), BF16),
            vmem((tokens, width), BF16),
            vmem(left_stat.shape, F32),
            vmem(right_stat.shape, F32),
            vmem(left_root.shape, BF16),
            vmem(right_root.shape, BF16),
            vmem((order, width), F32),
        ]
        + [vmem((4, slab, width), BF16)] * 4
        + [vmem((order, width), BF16)] * 2
        + [vmem((blocks, slab, order), BF16)] * 6
        + [dma((4,)), dma((CHUNKS, 2))]
        + [dma((2, 4))] * 2
        + [dma((4,))] * 4
        + [dma((2, 4))] * 4
        + [dma((2, 3))] * 2,
        compiler_params=pltpu.CompilerParams(
            collective_id=0, has_side_effects=True, vmem_limit_bytes=48 * 1024 * 1024
        ),
        cost_estimate=pl.CostEstimate(
            flops=2 * tokens * order * width, bytes_accessed=4 * tokens * order, transcendentals=0
        ),
    )(block_owner, acts, out_grads, left_stat, right_stat, left_root, right_root)


def solution(mesh):
    in_specs = (
        P("dp", None),
        P("dp", "mp"),
        P(),
        P("mp", "dp", None),
        P("mp", "dp", None),
        P("mp", "dp", None),
        P("mp", "dp", None),
    )
    out_specs = (P("dp", "mp"), P("mp", "dp", None), P("mp", "dp", None))
    local = fused_local if fits_fused(mesh.shape) else collective_local
    return jax.shard_map(local, mesh=mesh, in_specs=in_specs, out_specs=out_specs, check_vma=False)
```

```python
import functools

import jax
import jax.numpy as jnp
from jax import lax
from jax.experimental import pallas as pl
from jax.experimental.pallas import tpu as pltpu
from jax.sharding import PartitionSpec as P


def state_index(block_owner, capacity):
    block_count = block_owner.shape[0]
    column_ids = jnp.arange(block_count, dtype=jnp.int32)
    same_owner = block_owner[None, :] == block_owner[:, None]
    earlier = column_ids[None, :] < column_ids[:, None]
    slot_rank = jnp.sum((same_owner & earlier).astype(jnp.int32), axis=1)
    return block_owner * capacity + slot_rank


def owner_hits(target, owner_index, capacity):
    wanted = owner_index * capacity + jnp.arange(capacity, dtype=jnp.int32)
    return target[None, :] == wanted[:, None]


def gram_rows(own_rows, own_cols, whole_grad):
    left_part = jnp.einsum("sik,sjk->sij", own_rows, whole_grad, preferred_element_type=jnp.float32)
    right_part = jnp.einsum(
        "ski,skj->sij", own_cols, whole_grad, preferred_element_type=jnp.float32
    )
    return (left_part, right_part)


def precondition(root_rows, whole_grad, whole_right):
    left_part = jnp.einsum(
        "sik,skj->sij", root_rows, whole_grad, preferred_element_type=jnp.float32
    ).astype(jnp.bfloat16)
    return jnp.einsum(
        "sik,skj->sij", left_part, whole_right, preferred_element_type=jnp.float32
    ).astype(jnp.bfloat16)


def route_slots(slot_match, slots):
    picker = jnp.transpose(slot_match).astype(jnp.bfloat16)
    return jnp.einsum("ds,sij->dij", picker, slots, preferred_element_type=jnp.float32).astype(
        jnp.bfloat16
    )


def collective_local(acts, out_grads, block_owner, left_stat, right_stat, left_root, right_root):
    block_order = acts.shape[1]
    slab_rows = block_order // lax.axis_size("dp")
    capacity = left_stat.shape[0]
    target = state_index(block_owner, capacity)
    column_index = lax.axis_index("mp")
    slab_start = lax.axis_index("dp") * slab_rows
    my_owner = block_owner[column_index]
    own_grad = lax.psum_scatter(
        jnp.einsum("tr,tc->rc", acts, out_grads, preferred_element_type=jnp.float32),
        "dp",
        scatter_dimension=0,
        tiled=True,
    ).astype(jnp.bfloat16)
    slot_match = owner_hits(target, column_index, capacity)
    slot_used = jnp.any(slot_match, axis=1)
    slot_weights = slot_match.astype(jnp.float32)
    left_out = route_slots(slot_match, left_root)
    right_out = route_slots(slot_match, right_root)
    left_arrived, right_arrived = (
        lax.all_to_all(left_out, "mp", split_axis=0, concat_axis=0, tiled=True),
        lax.all_to_all(right_out, "mp", split_axis=0, concat_axis=0, tiled=True),
    )
    root_rows = lax.dynamic_index_in_dim(left_arrived, my_owner, 0, keepdims=True)
    right_rows = lax.dynamic_index_in_dim(right_arrived, my_owner, 0, keepdims=True)
    whole_grad, whole_right = (
        lax.all_gather(own_grad[None], "dp", axis=1, tiled=True),
        lax.all_gather(right_rows, "dp", axis=1, tiled=True),
    )
    own_cols = lax.dynamic_slice_in_dim(whole_grad, slab_start, slab_rows, 2)
    left_part, right_part = gram_rows(own_grad[None], own_cols, whole_grad)
    update = precondition(root_rows, whole_grad, whole_right)[0]
    owner_ids = jnp.arange(block_owner.shape[0], dtype=jnp.int32)
    send_mask = (owner_ids == my_owner)[:, None, None]
    left_send = jnp.where(send_mask, left_part, 0.0)
    right_send = jnp.where(send_mask, right_part, 0.0)
    left_every_gram, right_every_gram = (
        lax.all_to_all(
            left_send.astype(jnp.bfloat16), "mp", split_axis=0, concat_axis=0, tiled=True
        ).astype(left_send.dtype),
        lax.all_to_all(
            right_send.astype(jnp.bfloat16), "mp", split_axis=0, concat_axis=0, tiled=True
        ).astype(right_send.dtype),
    )
    left_gram = jnp.einsum(
        "sc,cij->sij", slot_weights, left_every_gram, precision=lax.Precision.HIGHEST
    )
    right_gram = jnp.einsum(
        "sc,cij->sij", slot_weights, right_every_gram, precision=lax.Precision.HIGHEST
    )
    keep_mask = slot_used[:, None, None]
    left_new = jnp.where(keep_mask, 0.8 * left_stat + 0.2 * (left_gram / block_order), left_stat)
    right_new = jnp.where(
        keep_mask, 0.8 * right_stat + 0.2 * (right_gram / block_order), right_stat
    )
    return (update, left_new, right_new)


MESH = pl.DeviceIdType.MESH
BF16 = jnp.bfloat16
F32 = jnp.float32
NN = (((1,), (0,)), ((), ()))
NT = (((1,), (1,)), ((), ()))
TN = (((0,), (0,)), ((), ()))
CHUNKS = 4


def fits_fused(sizes):
    return sizes["dp"] == 8 and sizes["mp"] == 4


def flip(index, bits):
    if bits == 0:
        return index
    if bits == 1:
        return index + 1 - 2 * lax.rem(index, 2)
    if bits == 2:
        return lax.rem(index + 2, 4)
    return 3 - index


def dot(a, b, dims):
    return lax.dot_general(a, b, dims, preferred_element_type=F32)


def fused_kernel(
    owner_ref, acts_hbm, outg_hbm, left_stat_hbm, right_stat_hbm, left_root_hbm, right_root_hbm,
    update_ref, left_new_ref, right_new_ref,
    acts, outg, lstat, rstat, lroot, rroot,
    part, send_x, recv_x, send_z, recv_z, grad, right,
    lout, rout, larr, rarr, lgram, rgram, gram_out, update_out,
    load_sem, tok_sem, route_ss, route_rs, rsx_ss, rsx_rs, rsz_ss, rsz_rs,
    agz_ss, agz_rs, agc_ss, agc_rs, gram_ss, gram_rs, fwd_ss, upd_ss, upd_rs,
):
    blocks = owner_ref.shape[0]
    order = part.shape[0]
    capacity, slab = lstat.shape[0], lstat.shape[1]
    half = order // 2
    chunk = acts.shape[0] // CHUNKS
    d, m = lax.axis_index("dp"), lax.axis_index("mp")
    z, x = d // 2, lax.rem(d, 2)
    y, k = m // 2, lax.rem(m, 2)
    turned = lax.rem(x + k, 2)
    work = y * 2 + x

    def device(zz, xx, yy, kk):
        return {"dp": zz * 2 + xx, "mp": yy * 2 + kk}

    def rows_of(zz, kk):
        return pl.ds(pl.multiple_of((zz * 2 + kk) * slab, slab), slab)

    def remote(src, dst, ss, rs, to):
        return pltpu.make_async_remote_copy(
            src_ref=src, dst_ref=dst, send_sem=ss, recv_sem=rs, device_id=to, device_id_type=MESH
        )

    loads = [
        pltpu.make_async_copy(right_root_hbm, rroot, load_sem.at[0]),
        pltpu.make_async_copy(left_root_hbm, lroot, load_sem.at[1]),
    ]
    for copy in loads:
        copy.start()
    tokens = []
    for t in range(CHUNKS):
        rows = pl.ds(t * chunk, chunk)
        pair = (
            pltpu.make_async_copy(acts_hbm.at[rows], acts.at[rows], tok_sem.at[t, 0]),
            pltpu.make_async_copy(outg_hbm.at[rows], outg.at[rows], tok_sem.at[t, 1]),
        )
        for copy in pair:
            copy.start()
        tokens.append(pair)
    stats = [
        pltpu.make_async_copy(left_stat_hbm, lstat, load_sem.at[2]),
        pltpu.make_async_copy(right_stat_hbm, rstat, load_sem.at[3]),
    ]
    for copy in stats:
        copy.start()

    barrier = pltpu.get_barrier_semaphore()
    partners = [{"dp": flip(z, j) * 2 + x, "mp": m} for j in (1, 2, 3)]
    partners += [
        {"dp": z * 2 + xx, "mp": flip(m, j)}
        for xx, j in [(x, 1), (x, 2), (x, 3)] + [(1 - x, j) for j in range(4)]
    ]
    for to in partners:
        pl.semaphore_signal(barrier, inc=1, device_id=to, device_id_type=MESH)

    owners = [owner_ref[c] for c in range(blocks)]

    def rank_of(c):
        own = owner_ref[c]
        rank = jnp.int32(0)
        for other in range(blocks):
            hit = jnp.logical_and(owners[other] == own, other < c)
            rank = rank + jnp.where(hit, 1, 0).astype(jnp.int32)
        return jnp.minimum(rank, capacity - 1)

    loads[0].wait()
    loads[1].wait()
    pl.semaphore_wait(barrier, len(partners))
    pending, pending_turned = [], []

    def start(copy):
        copy.start()
        pending.append(copy)
        return copy

    def route_copy(q, out, arr, j, source):
        c = flip(work, j)
        to = {"dp": z * 2 + lax.rem(c, 2), "mp": (c // 2) * 2 + x}
        return remote(out.at[j], arr.at[source], route_ss.at[q, j], route_rs.at[q, source], to)

    def route(q, root, out, arr):
        for j in (3, 1, 2):
            out[j] = root[rank_of(flip(work, j))]
            start(route_copy(q, out, arr, j, m))
        own = root[rank_of(work)]
        out[0] = own
        copy = route_copy(q, out, arr, 0, m)
        pending_turned.append(copy)

        @pl.when(turned == 1)
        def _():
            copy.start()

        @pl.when(turned == 0)
        def _():
            arr[m] = own

    def route_wait(q, out, arr):
        for source in range(blocks):

            @pl.when(jnp.logical_or(turned == 1, m != source))
            def _(source=source):
                route_copy(q, out, arr, 1, source).wait_recv()

    route(0, rroot, rout, rarr)

    part[...] = jnp.zeros_like(part)
    first_core = k * turned + (1 - k) * (1 - turned)

    def sum_x_copy(slot, into, j):
        to = device(z, k, y, first_core if slot == 0 else 1 - k)
        return remote(
            send_x.at[slot, j], recv_x.at[into, j], rsx_ss.at[slot, j], rsx_rs.at[into, j], to
        )

    for step in range(2):
        which = 1 - z // 2 if step == 0 else z // 2
        base = pl.multiple_of(which * half, half)
        if step == 0:
            for t in range(CHUNKS):
                for copy in tokens[t]:
                    copy.wait()

        def token_step(t, carry):
            rows = pl.ds(pl.multiple_of(t * chunk, chunk), chunk)
            part[pl.ds(base, half), :] += dot(acts[rows, pl.ds(base, half)], outg[rows, :], TN)
            return carry

        lax.fori_loop(0, CHUNKS, token_step, 0)
        for j in ((2, 3), (1, 0))[step]:
            send_x[0, j] = part[rows_of(flip(z, j), first_core), :].astype(BF16)
            start(sum_x_copy(0, turned, j))
            second = sum_x_copy(1, 1, j)
            pending_turned.append(second)

            @pl.when(turned == 1)
            def _(j=j, second=second):
                send_x[1, j] = part[rows_of(flip(z, j), 1 - k), :].astype(BF16)
                second.start()

    me = rows_of(z, k)
    beside = {"mp": flip(m, 1)}

    def gather_own(q, ref):
        copies = {
            "c0": start(remote(ref.at[me], ref.at[me], agc_ss.at[q, 0], agc_rs.at[q, 0], beside))
        }
        for j in (2, 3, 1):
            copies[j] = start(
                remote(
                    ref.at[me], ref.at[me], agz_ss.at[q, j], agz_rs.at[q, j],
                    {"dp": flip(z, j) * 2 + x},
                )
            )
        return copies

    def gather_on(q, ref, copies):
        for j in (1, 2, 3):
            copies[j].wait_recv()
            rows = rows_of(flip(z, j), k)
            copies["c%d" % j] = start(
                remote(ref.at[rows], ref.at[rows], agc_ss.at[q, j], agc_rs.at[q, j], beside)
            )

    route_wait(0, rout, rarr)
    right[me, :] = rarr[owner_ref[work]]
    right_copies = gather_own(1, right)

    sum_z = {}
    for j in (2, 3, 1, 0):
        rows = rows_of(flip(z, j), k)

        @pl.when(turned == 1)
        def _(j=j, rows=rows):
            sum_x_copy(0, 0, j).wait_recv()
            part[rows, :] = recv_x[0, j].astype(F32)

        sum_x_copy(0, 1, j).wait_recv()
        both = part[rows, :] + recv_x[1, j].astype(F32)
        if j == 0:
            total = both
        else:
            send_z[j] = both.astype(BF16)
            sum_z[j] = start(
                remote(
                    send_z.at[j], recv_z.at[j], rsz_ss.at[j], rsz_rs.at[j],
                    {"dp": flip(z, j) * 2 + x},
                )
            )
    route(1, lroot, lout, larr)
    for j in (1, 2, 3):
        sum_z[j].wait_recv()
        total = total + recv_z[j].astype(F32)
    own_grad = total.astype(BF16)
    grad[me, :] = own_grad
    copies = gather_own(0, grad)
    gather_on(1, right, right_copies)
    gather_on(0, grad, copies)
    for j in range(4):
        copies["c%d" % j].wait_recv()

    whole = grad[...]

    def gram_copy(q, way, block):
        ref = (lgram, rgram)[q]
        to = device(z, k, y, first_core) if way == 0 else device(z, k, 1 - y, k)
        return remote(gram_out.at[q], ref.at[block], gram_ss.at[q, way], gram_rs.at[q, block], to)

    def share(q, value):
        gram_out[q] = value
        start(gram_copy(q, 1, work))
        start(gram_copy(q, 0, work))

        @pl.when(turned == 0)
        def _():
            (lgram, rgram)[q][work] = value

    share(0, dot(own_grad, whole, NT).astype(BF16))
    row_ids = lax.broadcasted_iota(jnp.int32, (slab, order), 0)
    col_ids = lax.broadcasted_iota(jnp.int32, (slab, order), 1)
    picker = jnp.where(col_ids == row_ids + (z * 2 + k) * slab, 1.0, 0.0).astype(BF16)
    own_cols = dot(picker, whole, NT).astype(BF16)
    share(1, dot(own_cols, whole, NN).astype(BF16))
    route_wait(1, lout, larr)
    precond = dot(larr[owner_ref[work]], whole, NN).astype(BF16)
    for j in range(4):
        right_copies["c%d" % j].wait_recv()
    update = dot(precond, right[...], NN).astype(BF16)
    update_out[...] = update
    update_copy = remote(
        update_out, update_ref, upd_ss.at[0], upd_rs.at[0], device(z, k, y, x)
    )

    @pl.when(turned == 1)
    def _():
        update_copy.start()

    def forward_copy(q, j):
        ref, block = (lgram, rgram)[q], flip(work, j)
        return remote(ref.at[block], ref.at[block], fwd_ss.at[q, j], gram_rs.at[q, block], beside)

    @pl.when(turned == 0)
    def _():
        update_ref[...] = update
        for q in range(2):
            for j in (1, 2, 3):
                gram_copy(q, 0, flip(work, j)).wait_recv()
                forward_copy(q, j).start()

    @pl.when(turned == 1)
    def _():
        for q in range(2):
            for j in range(4):
                gram_copy(q, 0, flip(work, j)).wait_recv()

    picks = []
    for s in range(capacity):
        index, used = jnp.int32(0), jnp.int32(0)
        for c in range(blocks):
            hit = jnp.logical_and(owners[c] == m, rank_of(c) == s)
            index = index + jnp.where(hit, c, 0).astype(jnp.int32)
            used = used + jnp.where(hit, 1, 0).astype(jnp.int32)
        picks.append((jnp.minimum(index, blocks - 1), used))
    for q, (ref, stat, new) in enumerate(((lgram, lstat, left_new_ref), (rgram, rstat, right_new_ref))):
        stats[q].wait()
        for s, (index, used) in enumerate(picks):
            old = stat[s]
            fresh = 0.8 * old + 0.2 * (ref[index].astype(F32) / order)
            new[s] = jnp.where(used > 0, fresh, old)
    for copy in pending:
        copy.wait_send()

    @pl.when(turned == 0)
    def _():
        for q in range(2):
            for j in (1, 2, 3):
                forward_copy(q, j).wait_send()

    @pl.when(turned == 1)
    def _():
        for copy in pending_turned:
            copy.wait_send()
        update_copy.wait_send()
        update_copy.wait_recv()


def fused_local(acts, out_grads, block_owner, left_stat, right_stat, left_root, right_root):
    capacity, slab, order = left_stat.shape
    blocks = block_owner.shape[0]
    tokens = acts.shape[0]
    width = out_grads.shape[1]
    dma, vmem = pltpu.SemaphoreType.DMA, pltpu.VMEM
    any_spec = pl.BlockSpec(memory_space=pltpu.HBM)
    vmem_spec = pl.BlockSpec(memory_space=pltpu.VMEM)
    return pl.pallas_call(
        fused_kernel,
        out_shape=(
            jax.ShapeDtypeStruct((slab, width), BF16),
            jax.ShapeDtypeStruct(left_stat.shape, F32),
            jax.ShapeDtypeStruct(right_stat.shape, F32),
        ),
        in_specs=[pl.BlockSpec(memory_space=pltpu.SMEM)] + [any_spec] * 6,
        out_specs=(vmem_spec,) * 3,
        scratch_shapes=[
            vmem((tokens, order), BF16),
            vmem((tokens, width), BF16),
            vmem(left_stat.shape, F32),
            vmem(right_stat.shape, F32),
            vmem(left_root.shape, BF16),
            vmem(right_root.shape, BF16),
            vmem((order, width), F32),
        ]
        + [vmem((2, 4, slab, width), BF16)] * 2
        + [vmem((4, slab, width), BF16)] * 2
        + [vmem((order, width), BF16)] * 2
        + [vmem((blocks, slab, order), BF16)] * 6
        + [vmem((2, slab, order), BF16), vmem((slab, width), BF16)]
        + [dma((4,)), dma((CHUNKS, 2))]
        + [dma((2, 4))] * 4
        + [dma((4,))] * 2
        + [dma((2, 4))] * 4
        + [dma((2, 2)), dma((2, 4)), dma((2, 4)), dma((1,)), dma((1,))],
        compiler_params=pltpu.CompilerParams(
            collective_id=0, has_side_effects=True, vmem_limit_bytes=56 * 1024 * 1024
        ),
        cost_estimate=pl.CostEstimate(
            flops=2 * tokens * order * width, bytes_accessed=4 * tokens * order, transcendentals=0
        ),
    )(block_owner, acts, out_grads, left_stat, right_stat, left_root, right_root)


def solution(mesh):
    in_specs = (
        P("dp", None),
        P("dp", "mp"),
        P(),
        P("mp", "dp", None),
        P("mp", "dp", None),
        P("mp", "dp", None),
        P("mp", "dp", None),
    )
    out_specs = (P("dp", "mp"), P("mp", "dp", None), P("mp", "dp", None))
    local = fused_local if fits_fused(mesh.shape) else collective_local
    return jax.shard_map(local, mesh=mesh, in_specs=in_specs, out_specs=out_specs, check_vma=False)
```

```python
import functools

import jax
import jax.numpy as jnp
from jax import lax
from jax.experimental import pallas as pl
from jax.experimental.pallas import tpu as pltpu
from jax.sharding import PartitionSpec as P


def state_index(block_owner, capacity):
    block_count = block_owner.shape[0]
    column_ids = jnp.arange(block_count, dtype=jnp.int32)
    same_owner = block_owner[None, :] == block_owner[:, None]
    earlier = column_ids[None, :] < column_ids[:, None]
    slot_rank = jnp.sum((same_owner & earlier).astype(jnp.int32), axis=1)
    return block_owner * capacity + slot_rank


def owner_hits(target, owner_index, capacity):
    wanted = owner_index * capacity + jnp.arange(capacity, dtype=jnp.int32)
    return target[None, :] == wanted[:, None]


def gram_rows(own_rows, own_cols, whole_grad):
    left_part = jnp.einsum("sik,sjk->sij", own_rows, whole_grad, preferred_element_type=jnp.float32)
    right_part = jnp.einsum(
        "ski,skj->sij", own_cols, whole_grad, preferred_element_type=jnp.float32
    )
    return (left_part, right_part)


def precondition(root_rows, whole_grad, whole_right):
    left_part = jnp.einsum(
        "sik,skj->sij", root_rows, whole_grad, preferred_element_type=jnp.float32
    ).astype(jnp.bfloat16)
    return jnp.einsum(
        "sik,skj->sij", left_part, whole_right, preferred_element_type=jnp.float32
    ).astype(jnp.bfloat16)


def route_slots(slot_match, slots):
    picker = jnp.transpose(slot_match).astype(jnp.bfloat16)
    return jnp.einsum("ds,sij->dij", picker, slots, preferred_element_type=jnp.float32).astype(
        jnp.bfloat16
    )


def collective_local(acts, out_grads, block_owner, left_stat, right_stat, left_root, right_root):
    block_order = acts.shape[1]
    slab_rows = block_order // lax.axis_size("dp")
    capacity = left_stat.shape[0]
    target = state_index(block_owner, capacity)
    column_index = lax.axis_index("mp")
    slab_start = lax.axis_index("dp") * slab_rows
    my_owner = block_owner[column_index]
    own_grad = lax.psum_scatter(
        jnp.einsum("tr,tc->rc", acts, out_grads, preferred_element_type=jnp.float32),
        "dp",
        scatter_dimension=0,
        tiled=True,
    ).astype(jnp.bfloat16)
    slot_match = owner_hits(target, column_index, capacity)
    slot_used = jnp.any(slot_match, axis=1)
    slot_weights = slot_match.astype(jnp.float32)
    left_out = route_slots(slot_match, left_root)
    right_out = route_slots(slot_match, right_root)
    left_arrived, right_arrived = (
        lax.all_to_all(left_out, "mp", split_axis=0, concat_axis=0, tiled=True),
        lax.all_to_all(right_out, "mp", split_axis=0, concat_axis=0, tiled=True),
    )
    root_rows = lax.dynamic_index_in_dim(left_arrived, my_owner, 0, keepdims=True)
    right_rows = lax.dynamic_index_in_dim(right_arrived, my_owner, 0, keepdims=True)
    whole_grad, whole_right = (
        lax.all_gather(own_grad[None], "dp", axis=1, tiled=True),
        lax.all_gather(right_rows, "dp", axis=1, tiled=True),
    )
    own_cols = lax.dynamic_slice_in_dim(whole_grad, slab_start, slab_rows, 2)
    left_part, right_part = gram_rows(own_grad[None], own_cols, whole_grad)
    update = precondition(root_rows, whole_grad, whole_right)[0]
    owner_ids = jnp.arange(block_owner.shape[0], dtype=jnp.int32)
    send_mask = (owner_ids == my_owner)[:, None, None]
    left_send = jnp.where(send_mask, left_part, 0.0)
    right_send = jnp.where(send_mask, right_part, 0.0)
    left_every_gram, right_every_gram = (
        lax.all_to_all(
            left_send.astype(jnp.bfloat16), "mp", split_axis=0, concat_axis=0, tiled=True
        ).astype(left_send.dtype),
        lax.all_to_all(
            right_send.astype(jnp.bfloat16), "mp", split_axis=0, concat_axis=0, tiled=True
        ).astype(right_send.dtype),
    )
    left_gram = jnp.einsum(
        "sc,cij->sij", slot_weights, left_every_gram, precision=lax.Precision.HIGHEST
    )
    right_gram = jnp.einsum(
        "sc,cij->sij", slot_weights, right_every_gram, precision=lax.Precision.HIGHEST
    )
    keep_mask = slot_used[:, None, None]
    left_new = jnp.where(keep_mask, 0.8 * left_stat + 0.2 * (left_gram / block_order), left_stat)
    right_new = jnp.where(
        keep_mask, 0.8 * right_stat + 0.2 * (right_gram / block_order), right_stat
    )
    return (update, left_new, right_new)


MESH = pl.DeviceIdType.MESH
BF16 = jnp.bfloat16
F32 = jnp.float32
NN = (((1,), (0,)), ((), ()))
NT = (((1,), (1,)), ((), ()))
TN = (((0,), (0,)), ((), ()))
CHUNKS = 4


def fits_fused(sizes):
    return sizes["dp"] == 8 and sizes["mp"] == 4


def flip(index, bits):
    if bits == 0:
        return index
    if bits == 1:
        return index + 1 - 2 * lax.rem(index, 2)
    if bits == 2:
        return lax.rem(index + 2, 4)
    return 3 - index


def dot(a, b, dims):
    return lax.dot_general(a, b, dims, preferred_element_type=F32)


def fused_kernel(
    owner_ref, acts_hbm, outg_hbm, left_stat_hbm, right_stat_hbm, left_root_hbm, right_root_hbm,
    update_ref, left_new_ref, right_new_ref,
    acts, outg, lstat, rstat, lroot, rroot,
    part, send_x, recv_x, send_z, recv_z, grad, right,
    lout, rout, larr, rarr, lgram, rgram, gram_out, update_out,
    load_sem, tok_sem, route_ss, route_rs, rsx_ss, rsx_rs, rsz_ss, rsz_rs,
    agz_ss, agz_rs, agc_ss, agc_rs, gram_ss, gram_rs, fwd_ss, upd_ss, upd_rs,
):
    blocks = owner_ref.shape[0]
    order = part.shape[0]
    capacity, slab = lstat.shape[0], lstat.shape[1]
    half = order // 2
    chunk = acts.shape[0] // CHUNKS
    d, m = lax.axis_index("dp"), lax.axis_index("mp")
    z, x = d // 2, lax.rem(d, 2)
    y, k = m // 2, lax.rem(m, 2)
    turned = lax.rem(x + k, 2)
    work = y * 2 + x

    def device(zz, xx, yy, kk):
        return {"dp": zz * 2 + xx, "mp": yy * 2 + kk}

    def rows_of(zz, kk):
        return pl.ds(pl.multiple_of((zz * 2 + kk) * slab, slab), slab)

    def remote(src, dst, ss, rs, to):
        return pltpu.make_async_remote_copy(
            src_ref=src, dst_ref=dst, send_sem=ss, recv_sem=rs, device_id=to, device_id_type=MESH
        )

    loads = [
        pltpu.make_async_copy(right_root_hbm, rroot, load_sem.at[0]),
        pltpu.make_async_copy(left_root_hbm, lroot, load_sem.at[1]),
    ]
    for copy in loads:
        copy.start()
    tokens = []
    for t in range(CHUNKS):
        rows = pl.ds(t * chunk, chunk)
        pair = (
            pltpu.make_async_copy(acts_hbm.at[rows], acts.at[rows], tok_sem.at[t, 0]),
            pltpu.make_async_copy(outg_hbm.at[rows], outg.at[rows], tok_sem.at[t, 1]),
        )
        for copy in pair:
            copy.start()
        tokens.append(pair)
    stats = [
        pltpu.make_async_copy(left_stat_hbm, lstat, load_sem.at[2]),
        pltpu.make_async_copy(right_stat_hbm, rstat, load_sem.at[3]),
    ]
    for copy in stats:
        copy.start()

    barrier = pltpu.get_barrier_semaphore()
    partners = [{"dp": flip(z, j) * 2 + x, "mp": m} for j in (1, 2, 3)]
    partners += [
        {"dp": z * 2 + xx, "mp": flip(m, j)}
        for xx, j in [(x, 1), (x, 2), (x, 3)] + [(1 - x, j) for j in range(4)]
    ]
    for to in partners:
        pl.semaphore_signal(barrier, inc=1, device_id=to, device_id_type=MESH)

    owners = [owner_ref[c] for c in range(blocks)]

    def rank_of(c):
        own = owner_ref[c]
        rank = jnp.int32(0)
        for other in range(blocks):
            hit = jnp.logical_and(owners[other] == own, other < c)
            rank = rank + jnp.where(hit, 1, 0).astype(jnp.int32)
        return jnp.minimum(rank, capacity - 1)

    loads[0].wait()
    loads[1].wait()
    pl.semaphore_wait(barrier, len(partners))
    pending, pending_turned = [], []

    def start(copy):
        copy.start()
        pending.append(copy)
        return copy

    def route_copy(q, out, arr, j, source):
        c = flip(work, j)
        to = {"dp": z * 2 + lax.rem(c, 2), "mp": (c // 2) * 2 + x}
        return remote(out.at[j], arr.at[source], route_ss.at[q, j], route_rs.at[q, source], to)

    def route(q, root, out, arr):
        for j in (3, 1, 2):
            out[j] = root[rank_of(flip(work, j))]
            start(route_copy(q, out, arr, j, m))
        own = root[rank_of(work)]
        out[0] = own
        copy = route_copy(q, out, arr, 0, m)
        pending_turned.append(copy)

        @pl.when(turned == 1)
        def _():
            copy.start()

        @pl.when(turned == 0)
        def _():
            arr[m] = own

    def route_wait(q, out, arr):
        for source in range(blocks):

            @pl.when(jnp.logical_or(turned == 1, m != source))
            def _(source=source):
                route_copy(q, out, arr, 1, source).wait_recv()

    route(0, rroot, rout, rarr)

    part[...] = jnp.zeros_like(part)
    first_core = k * turned + (1 - k) * (1 - turned)

    def sum_x_copy(slot, into, j):
        to = device(z, k, y, first_core if slot == 0 else 1 - k)
        return remote(
            send_x.at[slot, j], recv_x.at[into, j], rsx_ss.at[slot, j], rsx_rs.at[into, j], to
        )

    for step in range(2):
        which = 1 - z // 2 if step == 0 else z // 2
        base = pl.multiple_of(which * half, half)
        if step == 0:
            for t in range(CHUNKS):
                for copy in tokens[t]:
                    copy.wait()

        def token_step(t, carry):
            rows = pl.ds(pl.multiple_of(t * chunk, chunk), chunk)
            part[pl.ds(base, half), :] += dot(acts[rows, pl.ds(base, half)], outg[rows, :], TN)
            return carry

        lax.fori_loop(0, CHUNKS, token_step, 0)
        for j in ((2, 3), (1, 0))[step]:
            send_x[0, j] = part[rows_of(flip(z, j), first_core), :].astype(BF16)
            start(sum_x_copy(0, turned, j))
            second = sum_x_copy(1, 1, j)
            pending_turned.append(second)

            @pl.when(turned == 1)
            def _(j=j, second=second):
                send_x[1, j] = part[rows_of(flip(z, j), 1 - k), :].astype(BF16)
                second.start()

    me = rows_of(z, k)
    beside = {"mp": flip(m, 1)}

    def gather_own(q, ref):
        copies = {
            "c0": start(remote(ref.at[me], ref.at[me], agc_ss.at[q, 0], agc_rs.at[q, 0], beside))
        }
        for j in (2, 3, 1):
            copies[j] = start(
                remote(
                    ref.at[me], ref.at[me], agz_ss.at[q, j], agz_rs.at[q, j],
                    {"dp": flip(z, j) * 2 + x},
                )
            )
        return copies

    def gather_on(q, ref, copies):
        for j in (1, 2, 3):
            copies[j].wait_recv()
            rows = rows_of(flip(z, j), k)
            copies["c%d" % j] = start(
                remote(ref.at[rows], ref.at[rows], agc_ss.at[q, j], agc_rs.at[q, j], beside)
            )

    route_wait(0, rout, rarr)
    right[me, :] = rarr[owner_ref[work]]

    sum_z = {}
    for j in (2, 3, 1, 0):
        rows = rows_of(flip(z, j), k)

        @pl.when(turned == 1)
        def _(j=j, rows=rows):
            sum_x_copy(0, 0, j).wait_recv()
            part[rows, :] = recv_x[0, j].astype(F32)

        sum_x_copy(0, 1, j).wait_recv()
        both = part[rows, :] + recv_x[1, j].astype(F32)
        if j == 0:
            total = both
        else:
            send_z[j] = both.astype(BF16)
            sum_z[j] = start(
                remote(
                    send_z.at[j], recv_z.at[j], rsz_ss.at[j], rsz_rs.at[j],
                    {"dp": flip(z, j) * 2 + x},
                )
            )
    route(1, lroot, lout, larr)
    for j in (1, 2, 3):
        sum_z[j].wait_recv()
        total = total + recv_z[j].astype(F32)
    own_grad = total.astype(BF16)
    grad[me, :] = own_grad
    copies = gather_own(0, grad)
    right_copies = gather_own(1, right)
    gather_on(0, grad, copies)
    for j in range(4):
        copies["c%d" % j].wait_recv()

    whole = grad[...]

    def gram_copy(q, way, block):
        ref = (lgram, rgram)[q]
        to = device(z, k, y, first_core) if way == 0 else device(z, k, 1 - y, k)
        return remote(gram_out.at[q], ref.at[block], gram_ss.at[q, way], gram_rs.at[q, block], to)

    def share(q, value):
        gram_out[q] = value
        start(gram_copy(q, 1, work))
        start(gram_copy(q, 0, work))

        @pl.when(turned == 0)
        def _():
            (lgram, rgram)[q][work] = value

    share(0, dot(own_grad, whole, NT).astype(BF16))
    row_ids = lax.broadcasted_iota(jnp.int32, (slab, order), 0)
    col_ids = lax.broadcasted_iota(jnp.int32, (slab, order), 1)
    picker = jnp.where(col_ids == row_ids + (z * 2 + k) * slab, 1.0, 0.0).astype(BF16)
    own_cols = dot(picker, whole, NT).astype(BF16)
    share(1, dot(own_cols, whole, NN).astype(BF16))
    gather_on(1, right, right_copies)
    route_wait(1, lout, larr)
    precond = dot(larr[owner_ref[work]], whole, NN).astype(BF16)
    def forward_copy(q, j):
        ref, block = (lgram, rgram)[q], flip(work, j)
        return remote(ref.at[block], ref.at[block], fwd_ss.at[q, j], gram_rs.at[q, block], beside)

    @pl.when(turned == 0)
    def _():
        for q in range(2):
            for j in (1, 2, 3):
                gram_copy(q, 0, flip(work, j)).wait_recv()
                forward_copy(q, j).start()

    for j in range(4):
        right_copies["c%d" % j].wait_recv()
    update = dot(precond, right[...], NN).astype(BF16)
    update_out[...] = update
    update_copy = remote(
        update_out, update_ref, upd_ss.at[0], upd_rs.at[0], device(z, k, y, x)
    )

    @pl.when(turned == 1)
    def _():
        update_copy.start()

    @pl.when(turned == 0)
    def _():
        update_ref[...] = update

    @pl.when(turned == 1)
    def _():
        for q in range(2):
            for j in range(4):
                gram_copy(q, 0, flip(work, j)).wait_recv()

    picks = []
    for s in range(capacity):
        index, used = jnp.int32(0), jnp.int32(0)
        for c in range(blocks):
            hit = jnp.logical_and(owners[c] == m, rank_of(c) == s)
            index = index + jnp.where(hit, c, 0).astype(jnp.int32)
            used = used + jnp.where(hit, 1, 0).astype(jnp.int32)
        picks.append((jnp.minimum(index, blocks - 1), used))
    for q, (ref, stat, new) in enumerate(((lgram, lstat, left_new_ref), (rgram, rstat, right_new_ref))):
        stats[q].wait()
        for s, (index, used) in enumerate(picks):
            old = stat[s]
            fresh = 0.8 * old + 0.2 * (ref[index].astype(F32) / order)
            new[s] = jnp.where(used > 0, fresh, old)
    for copy in pending:
        copy.wait_send()

    @pl.when(turned == 0)
    def _():
        for q in range(2):
            for j in (1, 2, 3):
                forward_copy(q, j).wait_send()

    @pl.when(turned == 1)
    def _():
        for copy in pending_turned:
            copy.wait_send()
        update_copy.wait_send()
        update_copy.wait_recv()


def fused_local(acts, out_grads, block_owner, left_stat, right_stat, left_root, right_root):
    capacity, slab, order = left_stat.shape
    blocks = block_owner.shape[0]
    tokens = acts.shape[0]
    width = out_grads.shape[1]
    dma, vmem = pltpu.SemaphoreType.DMA, pltpu.VMEM
    any_spec = pl.BlockSpec(memory_space=pltpu.HBM)
    vmem_spec = pl.BlockSpec(memory_space=pltpu.VMEM)
    return pl.pallas_call(
        fused_kernel,
        out_shape=(
            jax.ShapeDtypeStruct((slab, width), BF16),
            jax.ShapeDtypeStruct(left_stat.shape, F32),
            jax.ShapeDtypeStruct(right_stat.shape, F32),
        ),
        in_specs=[pl.BlockSpec(memory_space=pltpu.SMEM)] + [any_spec] * 6,
        out_specs=(vmem_spec,) * 3,
        scratch_shapes=[
            vmem((tokens, order), BF16),
            vmem((tokens, width), BF16),
            vmem(left_stat.shape, F32),
            vmem(right_stat.shape, F32),
            vmem(left_root.shape, BF16),
            vmem(right_root.shape, BF16),
            vmem((order, width), F32),
        ]
        + [vmem((2, 4, slab, width), BF16)] * 2
        + [vmem((4, slab, width), BF16)] * 2
        + [vmem((order, width), BF16)] * 2
        + [vmem((blocks, slab, order), BF16)] * 6
        + [vmem((2, slab, order), BF16), vmem((slab, width), BF16)]
        + [dma((4,)), dma((CHUNKS, 2))]
        + [dma((2, 4))] * 4
        + [dma((4,))] * 2
        + [dma((2, 4))] * 4
        + [dma((2, 2)), dma((2, 4)), dma((2, 4)), dma((1,)), dma((1,))],
        compiler_params=pltpu.CompilerParams(
            collective_id=0, has_side_effects=True, vmem_limit_bytes=56 * 1024 * 1024
        ),
        cost_estimate=pl.CostEstimate(
            flops=2 * tokens * order * width, bytes_accessed=4 * tokens * order, transcendentals=0
        ),
    )(block_owner, acts, out_grads, left_stat, right_stat, left_root, right_root)


def solution(mesh):
    in_specs = (
        P("dp", None),
        P("dp", "mp"),
        P(),
        P("mp", "dp", None),
        P("mp", "dp", None),
        P("mp", "dp", None),
        P("mp", "dp", None),
    )
    out_specs = (P("dp", "mp"), P("mp", "dp", None), P("mp", "dp", None))
    local = fused_local if fits_fused(mesh.shape) else collective_local
    return jax.shard_map(local, mesh=mesh, in_specs=in_specs, out_specs=out_specs, check_vma=False)
```

```python
import functools

import jax
import jax.numpy as jnp
from jax import lax
from jax.experimental import pallas as pl
from jax.experimental.pallas import tpu as pltpu
from jax.sharding import PartitionSpec as P


def state_index(block_owner, capacity):
    block_count = block_owner.shape[0]
    column_ids = jnp.arange(block_count, dtype=jnp.int32)
    same_owner = block_owner[None, :] == block_owner[:, None]
    earlier = column_ids[None, :] < column_ids[:, None]
    slot_rank = jnp.sum((same_owner & earlier).astype(jnp.int32), axis=1)
    return block_owner * capacity + slot_rank


def owner_hits(target, owner_index, capacity):
    wanted = owner_index * capacity + jnp.arange(capacity, dtype=jnp.int32)
    return target[None, :] == wanted[:, None]


def gram_rows(own_rows, own_cols, whole_grad):
    left_part = jnp.einsum("sik,sjk->sij", own_rows, whole_grad, preferred_element_type=jnp.float32)
    right_part = jnp.einsum(
        "ski,skj->sij", own_cols, whole_grad, preferred_element_type=jnp.float32
    )
    return (left_part, right_part)


def precondition(root_rows, whole_grad, whole_right):
    left_part = jnp.einsum(
        "sik,skj->sij", root_rows, whole_grad, preferred_element_type=jnp.float32
    ).astype(jnp.bfloat16)
    return jnp.einsum(
        "sik,skj->sij", left_part, whole_right, preferred_element_type=jnp.float32
    ).astype(jnp.bfloat16)


def route_slots(slot_match, slots):
    picker = jnp.transpose(slot_match).astype(jnp.bfloat16)
    return jnp.einsum("ds,sij->dij", picker, slots, preferred_element_type=jnp.float32).astype(
        jnp.bfloat16
    )


def collective_local(acts, out_grads, block_owner, left_stat, right_stat, left_root, right_root):
    block_order = acts.shape[1]
    slab_rows = block_order // lax.axis_size("dp")
    capacity = left_stat.shape[0]
    target = state_index(block_owner, capacity)
    column_index = lax.axis_index("mp")
    slab_start = lax.axis_index("dp") * slab_rows
    my_owner = block_owner[column_index]
    own_grad = lax.psum_scatter(
        jnp.einsum("tr,tc->rc", acts, out_grads, preferred_element_type=jnp.float32),
        "dp",
        scatter_dimension=0,
        tiled=True,
    ).astype(jnp.bfloat16)
    slot_match = owner_hits(target, column_index, capacity)
    slot_used = jnp.any(slot_match, axis=1)
    slot_weights = slot_match.astype(jnp.float32)
    left_out = route_slots(slot_match, left_root)
    right_out = route_slots(slot_match, right_root)
    left_arrived, right_arrived = (
        lax.all_to_all(left_out, "mp", split_axis=0, concat_axis=0, tiled=True),
        lax.all_to_all(right_out, "mp", split_axis=0, concat_axis=0, tiled=True),
    )
    root_rows = lax.dynamic_index_in_dim(left_arrived, my_owner, 0, keepdims=True)
    right_rows = lax.dynamic_index_in_dim(right_arrived, my_owner, 0, keepdims=True)
    whole_grad, whole_right = (
        lax.all_gather(own_grad[None], "dp", axis=1, tiled=True),
        lax.all_gather(right_rows, "dp", axis=1, tiled=True),
    )
    own_cols = lax.dynamic_slice_in_dim(whole_grad, slab_start, slab_rows, 2)
    left_part, right_part = gram_rows(own_grad[None], own_cols, whole_grad)
    update = precondition(root_rows, whole_grad, whole_right)[0]
    owner_ids = jnp.arange(block_owner.shape[0], dtype=jnp.int32)
    send_mask = (owner_ids == my_owner)[:, None, None]
    left_send = jnp.where(send_mask, left_part, 0.0)
    right_send = jnp.where(send_mask, right_part, 0.0)
    left_every_gram, right_every_gram = (
        lax.all_to_all(
            left_send.astype(jnp.bfloat16), "mp", split_axis=0, concat_axis=0, tiled=True
        ).astype(left_send.dtype),
        lax.all_to_all(
            right_send.astype(jnp.bfloat16), "mp", split_axis=0, concat_axis=0, tiled=True
        ).astype(right_send.dtype),
    )
    left_gram = jnp.einsum(
        "sc,cij->sij", slot_weights, left_every_gram, precision=lax.Precision.HIGHEST
    )
    right_gram = jnp.einsum(
        "sc,cij->sij", slot_weights, right_every_gram, precision=lax.Precision.HIGHEST
    )
    keep_mask = slot_used[:, None, None]
    left_new = jnp.where(keep_mask, 0.8 * left_stat + 0.2 * (left_gram / block_order), left_stat)
    right_new = jnp.where(
        keep_mask, 0.8 * right_stat + 0.2 * (right_gram / block_order), right_stat
    )
    return (update, left_new, right_new)


MESH = pl.DeviceIdType.MESH
BF16 = jnp.bfloat16
F32 = jnp.float32
NN = (((1,), (0,)), ((), ()))
NT = (((1,), (1,)), ((), ()))
TN = (((0,), (0,)), ((), ()))
CHUNKS = 4


def fits_fused(sizes):
    return sizes["dp"] == 8 and sizes["mp"] == 4


def flip(index, bits):
    if bits == 0:
        return index
    if bits == 1:
        return index + 1 - 2 * lax.rem(index, 2)
    if bits == 2:
        return lax.rem(index + 2, 4)
    return 3 - index


def dot(a, b, dims):
    return lax.dot_general(a, b, dims, preferred_element_type=F32)


def fused_kernel(
    owner_ref, acts_hbm, outg_hbm, left_stat_hbm, right_stat_hbm, left_root_hbm, right_root_hbm,
    update_ref, left_new_ref, right_new_ref,
    acts, outg, lstat, rstat, lroot, rroot,
    part, send_x, recv_x, send_z, recv_z, grad, right,
    lout, rout, larr, rarr, lgram, rgram, gram_out, update_out,
    load_sem, tok_sem, route_ss, route_rs, rsx_ss, rsx_rs, rsz_ss, rsz_rs,
    agz_ss, agz_rs, agc_ss, agc_rs, gram_ss, gram_rs, fwd_ss, upd_ss, upd_rs,
):
    blocks = owner_ref.shape[0]
    order = part.shape[0]
    capacity, slab = lstat.shape[0], lstat.shape[1]
    half = order // 2
    chunk = acts.shape[0] // CHUNKS
    d, m = lax.axis_index("dp"), lax.axis_index("mp")
    z, x = d // 2, lax.rem(d, 2)
    y, k = m // 2, lax.rem(m, 2)
    turned = lax.rem(x + k, 2)
    work = y * 2 + x

    def device(zz, xx, yy, kk):
        return {"dp": zz * 2 + xx, "mp": yy * 2 + kk}

    def rows_of(zz, kk):
        return pl.ds(pl.multiple_of((zz * 2 + kk) * slab, slab), slab)

    def remote(src, dst, ss, rs, to):
        return pltpu.make_async_remote_copy(
            src_ref=src, dst_ref=dst, send_sem=ss, recv_sem=rs, device_id=to, device_id_type=MESH
        )

    loads = [
        pltpu.make_async_copy(right_root_hbm, rroot, load_sem.at[0]),
        pltpu.make_async_copy(left_root_hbm, lroot, load_sem.at[1]),
    ]
    for copy in loads:
        copy.start()
    tokens = []
    for t in range(CHUNKS):
        rows = pl.ds(t * chunk, chunk)
        pair = (
            pltpu.make_async_copy(acts_hbm.at[rows], acts.at[rows], tok_sem.at[t, 0]),
            pltpu.make_async_copy(outg_hbm.at[rows], outg.at[rows], tok_sem.at[t, 1]),
        )
        for copy in pair:
            copy.start()
        tokens.append(pair)
    stats = [
        pltpu.make_async_copy(left_stat_hbm, lstat, load_sem.at[2]),
        pltpu.make_async_copy(right_stat_hbm, rstat, load_sem.at[3]),
    ]
    for copy in stats:
        copy.start()

    barrier = pltpu.get_barrier_semaphore()
    partners = [{"dp": flip(z, j) * 2 + x, "mp": m} for j in (1, 2, 3)]
    partners += [
        {"dp": z * 2 + xx, "mp": flip(m, j)}
        for xx, j in [(x, 1), (x, 2), (x, 3)] + [(1 - x, j) for j in range(4)]
    ]
    for to in partners:
        pl.semaphore_signal(barrier, inc=1, device_id=to, device_id_type=MESH)

    owners = [owner_ref[c] for c in range(blocks)]

    def rank_of(c):
        own = owner_ref[c]
        rank = jnp.int32(0)
        for other in range(blocks):
            hit = jnp.logical_and(owners[other] == own, other < c)
            rank = rank + jnp.where(hit, 1, 0).astype(jnp.int32)
        return jnp.minimum(rank, capacity - 1)

    pl.semaphore_wait(barrier, len(partners))
    pending, pending_turned = [], []

    def start(copy):
        copy.start()
        pending.append(copy)
        return copy

    def route_copy(q, out, arr, j, source):
        c = flip(work, j)
        to = {"dp": z * 2 + lax.rem(c, 2), "mp": (c // 2) * 2 + x}
        return remote(out.at[j], arr.at[source], route_ss.at[q, j], route_rs.at[q, source], to)

    def route(q, root, out, arr):
        for j in (3, 1, 2):
            out[j] = root[rank_of(flip(work, j))]
            start(route_copy(q, out, arr, j, m))
        own = root[rank_of(work)]
        out[0] = own
        copy = route_copy(q, out, arr, 0, m)
        pending_turned.append(copy)

        @pl.when(turned == 1)
        def _():
            copy.start()

        @pl.when(turned == 0)
        def _():
            arr[m] = own

    def route_wait(q, out, arr):
        for source in range(blocks):

            @pl.when(jnp.logical_or(turned == 1, m != source))
            def _(source=source):
                route_copy(q, out, arr, 1, source).wait_recv()


    part[...] = jnp.zeros_like(part)
    first_core = k * turned + (1 - k) * (1 - turned)

    def sum_x_copy(slot, into, j):
        to = device(z, k, y, first_core if slot == 0 else 1 - k)
        return remote(
            send_x.at[slot, j], recv_x.at[into, j], rsx_ss.at[slot, j], rsx_rs.at[into, j], to
        )

    for step in range(2):
        which = 1 - z // 2 if step == 0 else z // 2
        base = pl.multiple_of(which * half, half)
        if step == 0:
            for t in range(CHUNKS):
                for copy in tokens[t]:
                    copy.wait()

        def token_step(t, carry):
            rows = pl.ds(pl.multiple_of(t * chunk, chunk), chunk)
            part[pl.ds(base, half), :] += dot(acts[rows, pl.ds(base, half)], outg[rows, :], TN)
            return carry

        lax.fori_loop(0, CHUNKS, token_step, 0)
        for j in ((2, 3), (1, 0))[step]:
            send_x[0, j] = part[rows_of(flip(z, j), first_core), :].astype(BF16)
            start(sum_x_copy(0, turned, j))
            second = sum_x_copy(1, 1, j)
            pending_turned.append(second)

            @pl.when(turned == 1)
            def _(j=j, second=second):
                send_x[1, j] = part[rows_of(flip(z, j), 1 - k), :].astype(BF16)
                second.start()

    me = rows_of(z, k)
    beside = {"mp": flip(m, 1)}

    def gather_own(q, ref):
        copies = {
            "c0": start(remote(ref.at[me], ref.at[me], agc_ss.at[q, 0], agc_rs.at[q, 0], beside))
        }
        for j in (2, 3, 1):
            copies[j] = start(
                remote(
                    ref.at[me], ref.at[me], agz_ss.at[q, j], agz_rs.at[q, j],
                    {"dp": flip(z, j) * 2 + x},
                )
            )
        return copies

    def gather_on(q, ref, copies):
        for j in (1, 2, 3):
            copies[j].wait_recv()
            rows = rows_of(flip(z, j), k)
            copies["c%d" % j] = start(
                remote(ref.at[rows], ref.at[rows], agc_ss.at[q, j], agc_rs.at[q, j], beside)
            )


    sum_z = {}
    for j in (2, 3, 1, 0):
        rows = rows_of(flip(z, j), k)

        @pl.when(turned == 1)
        def _(j=j, rows=rows):
            sum_x_copy(0, 0, j).wait_recv()
            part[rows, :] = recv_x[0, j].astype(F32)

        sum_x_copy(0, 1, j).wait_recv()
        both = part[rows, :] + recv_x[1, j].astype(F32)
        if j == 0:
            total = both
        else:
            send_z[j] = both.astype(BF16)
            sum_z[j] = start(
                remote(
                    send_z.at[j], recv_z.at[j], rsz_ss.at[j], rsz_rs.at[j],
                    {"dp": flip(z, j) * 2 + x},
                )
            )
    loads[0].wait()
    loads[1].wait()
    route(0, rroot, rout, rarr)
    route(1, lroot, lout, larr)
    for j in (1, 2, 3):
        sum_z[j].wait_recv()
        total = total + recv_z[j].astype(F32)
    own_grad = total.astype(BF16)
    grad[me, :] = own_grad
    copies = gather_own(0, grad)
    route_wait(0, rout, rarr)
    right[me, :] = rarr[owner_ref[work]]
    right_copies = gather_own(1, right)
    gather_on(0, grad, copies)
    for j in range(4):
        copies["c%d" % j].wait_recv()

    whole = grad[...]

    def gram_copy(q, way, block):
        ref = (lgram, rgram)[q]
        to = device(z, k, y, first_core) if way == 0 else device(z, k, 1 - y, k)
        return remote(gram_out.at[q], ref.at[block], gram_ss.at[q, way], gram_rs.at[q, block], to)

    def share(q, value):
        gram_out[q] = value
        start(gram_copy(q, 1, work))
        start(gram_copy(q, 0, work))

        @pl.when(turned == 0)
        def _():
            (lgram, rgram)[q][work] = value

    share(0, dot(own_grad, whole, NT).astype(BF16))
    row_ids = lax.broadcasted_iota(jnp.int32, (slab, order), 0)
    col_ids = lax.broadcasted_iota(jnp.int32, (slab, order), 1)
    picker = jnp.where(col_ids == row_ids + (z * 2 + k) * slab, 1.0, 0.0).astype(BF16)
    own_cols = dot(picker, whole, NT).astype(BF16)
    share(1, dot(own_cols, whole, NN).astype(BF16))
    gather_on(1, right, right_copies)
    route_wait(1, lout, larr)
    precond = dot(larr[owner_ref[work]], whole, NN).astype(BF16)
    def forward_copy(q, j):
        ref, block = (lgram, rgram)[q], flip(work, j)
        return remote(ref.at[block], ref.at[block], fwd_ss.at[q, j], gram_rs.at[q, block], beside)

    @pl.when(turned == 0)
    def _():
        for q in range(2):
            for j in (1, 2, 3):
                gram_copy(q, 0, flip(work, j)).wait_recv()
                forward_copy(q, j).start()

    for j in range(4):
        right_copies["c%d" % j].wait_recv()
    update = dot(precond, right[...], NN).astype(BF16)
    update_out[...] = update
    update_copy = remote(
        update_out, update_ref, upd_ss.at[0], upd_rs.at[0], device(z, k, y, x)
    )

    @pl.when(turned == 1)
    def _():
        update_copy.start()

    @pl.when(turned == 0)
    def _():
        update_ref[...] = update

    @pl.when(turned == 1)
    def _():
        for q in range(2):
            for j in range(4):
                gram_copy(q, 0, flip(work, j)).wait_recv()

    picks = []
    for s in range(capacity):
        index, used = jnp.int32(0), jnp.int32(0)
        for c in range(blocks):
            hit = jnp.logical_and(owners[c] == m, rank_of(c) == s)
            index = index + jnp.where(hit, c, 0).astype(jnp.int32)
            used = used + jnp.where(hit, 1, 0).astype(jnp.int32)
        picks.append((jnp.minimum(index, blocks - 1), used))
    for q, (ref, stat, new) in enumerate(((lgram, lstat, left_new_ref), (rgram, rstat, right_new_ref))):
        stats[q].wait()
        for s, (index, used) in enumerate(picks):
            old = stat[s]
            fresh = 0.8 * old + 0.2 * (ref[index].astype(F32) / order)
            new[s] = jnp.where(used > 0, fresh, old)
    for copy in pending:
        copy.wait_send()

    @pl.when(turned == 0)
    def _():
        for q in range(2):
            for j in (1, 2, 3):
                forward_copy(q, j).wait_send()

    @pl.when(turned == 1)
    def _():
        for copy in pending_turned:
            copy.wait_send()
        update_copy.wait_send()
        update_copy.wait_recv()


def fused_local(acts, out_grads, block_owner, left_stat, right_stat, left_root, right_root):
    capacity, slab, order = left_stat.shape
    blocks = block_owner.shape[0]
    tokens = acts.shape[0]
    width = out_grads.shape[1]
    dma, vmem = pltpu.SemaphoreType.DMA, pltpu.VMEM
    any_spec = pl.BlockSpec(memory_space=pltpu.HBM)
    vmem_spec = pl.BlockSpec(memory_space=pltpu.VMEM)
    return pl.pallas_call(
        fused_kernel,
        out_shape=(
            jax.ShapeDtypeStruct((slab, width), BF16),
            jax.ShapeDtypeStruct(left_stat.shape, F32),
            jax.ShapeDtypeStruct(right_stat.shape, F32),
        ),
        in_specs=[pl.BlockSpec(memory_space=pltpu.SMEM)] + [any_spec] * 6,
        out_specs=(vmem_spec,) * 3,
        scratch_shapes=[
            vmem((tokens, order), BF16),
            vmem((tokens, width), BF16),
            vmem(left_stat.shape, F32),
            vmem(right_stat.shape, F32),
            vmem(left_root.shape, BF16),
            vmem(right_root.shape, BF16),
            vmem((order, width), F32),
        ]
        + [vmem((2, 4, slab, width), BF16)] * 2
        + [vmem((4, slab, width), BF16)] * 2
        + [vmem((order, width), BF16)] * 2
        + [vmem((blocks, slab, order), BF16)] * 6
        + [vmem((2, slab, order), BF16), vmem((slab, width), BF16)]
        + [dma((4,)), dma((CHUNKS, 2))]
        + [dma((2, 4))] * 4
        + [dma((4,))] * 2
        + [dma((2, 4))] * 4
        + [dma((2, 2)), dma((2, 4)), dma((2, 4)), dma((1,)), dma((1,))],
        compiler_params=pltpu.CompilerParams(
            collective_id=0, has_side_effects=True, vmem_limit_bytes=56 * 1024 * 1024
        ),
        cost_estimate=pl.CostEstimate(
            flops=2 * tokens * order * width, bytes_accessed=4 * tokens * order, transcendentals=0
        ),
    )(block_owner, acts, out_grads, left_stat, right_stat, left_root, right_root)


def solution(mesh):
    in_specs = (
        P("dp", None),
        P("dp", "mp"),
        P(),
        P("mp", "dp", None),
        P("mp", "dp", None),
        P("mp", "dp", None),
        P("mp", "dp", None),
    )
    out_specs = (P("dp", "mp"), P("mp", "dp", None), P("mp", "dp", None))
    local = fused_local if fits_fused(mesh.shape) else collective_local
    return jax.shard_map(local, mesh=mesh, in_specs=in_specs, out_specs=out_specs, check_vma=False)
```
